32 devices in a mesh: inst: 4 (over z), scen: 8 (over y, x, core).
Axes of the slice: x: 2, y: 2, z: 4, core: 2. Of those that a mesh axis runs over, the one named last changes fastest.
Arguments:
- factor_returns: bfloat16 [8192, 64], P('scen'), may hold values from -0.8984375 to 0.8984375
- betas: bfloat16 [4000, 128], P('inst'), may hold values from -0.75 to 0.75
- base_state: bfloat16 [2, 4000], P(None, 'inst'), may hold values from 0.19921875 to 1
- underlying_slot: int32 [4000], replicated, may hold values from 0 to 3999, as said below
- chain_map: int32 [4096], replicated, may hold values from 0 to 3999, as said below
- strike_index: int32 [4096], P('inst'), may hold values from -8 to 8
- expiry: float32 [4096], P('inst'), may hold values from 0.05 to 2
- positions: int32 [1024, 4096], P(None, 'inst'), may hold values from -8 to 8
Outputs:
- losses: float32 [1024, 8192], P('inst', 'scen')
- margin: float32 [1024], P('inst')
The draws below stay inside these ranges and needn't reach their ends.
Inputs may be any that keep to these rules, and one draw needn't show every extreme that they name: A permutation: underlying u's loadings and base state stand in row underlying_slot[u]; rows k * 1000 to (k + 1) * 1000 - 1 form owner block k. `chain_map`: the options of each block of 1024 consecutive options name, among the underlyings whose slots lie in any one owner block of 1000 slots, at most 48 distinct underlyings; in every block of options exactly 48 for some owner block. Options of one underlying stand next to each other within a block.
All inputs are finite; a program needn't handle non-finite values.
Results may differ from the reference program's by a relative error of at most 0.02.
Values may be sent and summed in bfloat16 or wider, within the bound.
A program may use at most 64 MiB of HBM per device.

```python
import math
import jax
import jax.numpy as jnp
from jax import lax

U = 4000
F = 64
A = 1024
OPT_DEV = 1024
CAP = 48
S = 8192
OPTIONS = 4096


def chain_plan(key):
    inst_count = OPTIONS // OPT_DEV
    owner_rows = U // inst_count
    slot_order = jax.random.permutation(jax.random.fold_in(key, 11), U).astype(jnp.int32)
    owner_at = jnp.zeros((U,), jnp.int32).at[slot_order].set(jnp.arange(U, dtype=jnp.int32))
    lowest = max(1, CAP // 4)
    wanted = jax.random.randint(jax.random.fold_in(key, 12), (inst_count, inst_count), lowest, CAP + 1)
    full_owner = jax.random.randint(jax.random.fold_in(key, 13), (inst_count,), 0, inst_count)
    wanted = jnp.where(jnp.arange(inst_count)[None, :] == full_owner[:, None], CAP, wanted)
    scores = jax.random.randint(jax.random.fold_in(key, 14), (inst_count, inst_count, owner_rows), 0, 1 << 20)
    scores = scores * owner_rows + jnp.arange(owner_rows, dtype=jnp.int32)
    picks = jnp.argsort(scores, axis=-1)[:, :, :CAP].astype(jnp.int32)
    position = jnp.arange(OPT_DEV, dtype=jnp.int32)
    covering = position < inst_count * CAP
    first_owner = jnp.minimum(position // CAP, inst_count - 1)
    first_pick = position % CAP
    extra_owner = jax.random.randint(jax.random.fold_in(key, 15), (inst_count, OPT_DEV), 0, inst_count)
    owner_pick = jnp.where(covering[None, :], first_owner[None, :], extra_owner)
    limit = jnp.take_along_axis(wanted, owner_pick, axis=1)
    draw_first = jax.random.randint(jax.random.fold_in(key, 16), (inst_count, OPT_DEV), 0, limit)
    draw_second = jax.random.randint(jax.random.fold_in(key, 17), (inst_count, OPT_DEV), 0, limit)
    extra_pick = jnp.minimum(draw_first, draw_second)
    slot_pick = jnp.where(covering[None, :], first_pick[None, :] % limit, extra_pick)
    device_rows = jnp.arange(inst_count, dtype=jnp.int32)[:, None]
    local_row = picks[device_rows, owner_pick, slot_pick]
    slots = owner_pick * owner_rows + local_row
    underlying = jnp.sort(owner_at[slots], axis=1)
    return (slot_order, underlying.reshape(-1).astype(jnp.int32))


def draw_underlying_slot(key, part):
    return chain_plan(key)[0]


def draw_chain_map(key, part):
    return chain_plan(key)[1]


def place_ends(values, key, smallest, high):
    index_at = [jax.random.randint(jax.random.fold_in(key, axis), (), 0, length) for axis, length in enumerate(values.shape)]
    widest = values.shape.index(max(values.shape))
    beside = index_at[:widest] + [(index_at[widest] + 1) % values.shape[widest]] + index_at[widest + 1:]
    return values.at[tuple(index_at)].set(smallest).at[tuple(beside)].set(high)


def block_levels(stream_key, dims, cuts, smallest, largest):
    def one(axis_at, blocks):
        steps = jax.random.uniform(jax.random.fold_in(jax.random.fold_in(stream_key, 6), axis_at), (blocks,), jnp.float32, smallest / len(cuts), largest / len(cuts))
        return jnp.repeat(jnp.exp(steps), dims[axis_at] // blocks).reshape((-1,) + (1,) * (len(dims) - axis_at - 1))

    factor_of = one(*cuts[0])
    for cut in cuts[1:]:
        factor_of = factor_of * one(*cut)
    return factor_of


def gaussian(stream_key, extent, scale, bound, cuts=(), held_as=jnp.bfloat16):
    loudness = block_levels(stream_key, extent, cuts, -0.22, 0.18) if cuts else 1.0
    array = jax.random.normal(stream_key, extent, jnp.float32) * scale * loudness
    return jnp.minimum(jnp.maximum(array, -bound), bound).astype(held_as)


def setup_inputs(seed: int = 0) -> dict:
    splits = jax.random.split(jax.random.key(seed), 9)
    factor_returns = gaussian(splits[0], (S, F), 0.15, 0.8984375, ((0, 8),))
    betas = gaussian(splits[1], (U, 2 * F), F ** -0.5, 0.75, ((0, 4),))
    base_state = jnp.clip(jnp.exp(math.log(1.0) - 1.6133518 * jax.random.uniform(splits[2], (2, U), jnp.float32) ** block_levels(splits[2], (2, U), ((1, 4),), -0.2, 0.2)), 0.19921875, 1.0).astype(jnp.bfloat16)
    underlying_slot = draw_underlying_slot(jax.random.fold_in(splits[8], 71), 0)
    chain_map = draw_chain_map(jax.random.fold_in(splits[8], 71), 0)
    strike_index = place_ends(jax.random.randint(splits[5], (OPTIONS,), -8, 9), jax.random.fold_in(splits[5], 1), -8, 8).astype(jnp.int32)
    expiry = jnp.clip(jnp.exp(math.log(2.0) - 3.6888794 * jax.random.uniform(splits[6], (OPTIONS,), jnp.float32) ** block_levels(splits[6], (OPTIONS,), ((0, 4),), -0.2, 0.2)), 0.05, 2.0)
    positions = place_ends(jax.random.randint(splits[7], (A, OPTIONS), -8, 9), jax.random.fold_in(splits[7], 1), -8, 8).astype(jnp.int32)
    return dict(factor_returns=factor_returns, betas=betas, base_state=base_state, underlying_slot=underlying_slot, chain_map=chain_map, strike_index=strike_index, expiry=expiry, positions=positions)


strike_step = 0.05
contract_size = 0.03125

def normal_cdf(points):
    return 0.5 * lax.erfc(-points * 0.7071067811865476)

def option_value(forward, volatility, strike_level, expiry, call_flags):
    spread = volatility * jnp.sqrt(expiry)
    upper_arg = (jnp.log(forward / strike_level) + 0.5 * spread * spread) / spread
    lower_arg = upper_arg - spread
    call_value = forward * normal_cdf(upper_arg) - strike_level * normal_cdf(lower_arg)
    put_value = strike_level * normal_cdf(-lower_arg) - forward * normal_cdf(-upper_arg)
    return jnp.where(call_flags, call_value, put_value)

def reference(factor_returns, betas, base_state, underlying_slot, chain_map, strike_index, expiry, positions):
    shock_price = jnp.dot(betas[:, :F], factor_returns.T, preferred_element_type=jnp.float32)
    shock_vol = jnp.dot(betas[:, F:], factor_returns.T, preferred_element_type=jnp.float32)
    base_forward = base_state[0].astype(jnp.float32)
    base_vol = base_state[1].astype(jnp.float32)
    scen_forward = (base_forward[:, None] * jnp.exp(shock_price)).astype(jnp.bfloat16)
    scen_vol = (base_vol[:, None] * jnp.exp(shock_vol)).astype(jnp.bfloat16)
    all_slots = underlying_slot[chain_map].astype(jnp.int32)
    block_count = chain_map.shape[0] // OPT_DEV

    def one_block(running_sum, block_index):
        row_start = (block_index * OPT_DEV).astype(jnp.int32)
        block_slots = lax.dynamic_slice_in_dim(all_slots, row_start, OPT_DEV)
        strike_codes = lax.dynamic_slice_in_dim(strike_index, row_start, OPT_DEV)
        block_expiry = lax.dynamic_slice_in_dim(expiry, row_start, OPT_DEV)[:, None]
        forward = scen_forward[block_slots].astype(jnp.float32)
        volatility = scen_vol[block_slots].astype(jnp.float32)
        forward_zero = base_forward[block_slots][:, None]
        vol_zero = base_vol[block_slots][:, None]
        strike_level = forward_zero * jnp.exp(strike_step * strike_codes.astype(jnp.float32))[:, None]
        call_flags = (strike_codes >= 0)[:, None]
        scen_value = option_value(forward, volatility, strike_level, block_expiry, call_flags)
        base_value = option_value(forward_zero, vol_zero, strike_level, block_expiry, call_flags)
        profit = (scen_value - base_value).astype(jnp.bfloat16)
        held_counts = lax.dynamic_slice_in_dim(positions, row_start, OPT_DEV, 1).astype(jnp.bfloat16)
        partial_term = (contract_size * jnp.dot(held_counts, profit, preferred_element_type=jnp.float32)).astype(jnp.bfloat16)
        partial_term = lax.optimization_barrier(partial_term)
        return (running_sum + partial_term.astype(jnp.float32), None)
    start_sum = jnp.zeros((positions.shape[0], factor_returns.shape[0]), jnp.float32)
    losses, _ = lax.scan(one_block, start_sum, jnp.arange(block_count, dtype=jnp.int32))
    margin = lax.optimization_barrier(jnp.max(losses, axis=1))
    return (losses, margin)
```

```python
import functools
import jax
import jax.numpy as jnp
from jax import lax
from jax.experimental import pallas as pl
from jax.experimental.pallas import tpu as pltpu
from jax.sharding import PartitionSpec as P

F = 64
CAP = 48
strike_step = 0.05
contract_size = 0.03125
ERF_Q = (1.1283797055307927, 0.10276548081347335, -0.0001843820436491351, -0.0006257211496349986, 8.971323300994763e-05, -5.9858035855426975e-06, 1.5896701753059672e-07)
SQRT_HALF = 0.7071067811865476


def erf_points(points):
    square = jnp.minimum(points * points, 16.0)
    poly = ERF_Q[-1]
    for coef in ERF_Q[-2::-1]:
        poly = poly * square + coef
    return jnp.tanh(points * poly)


def split_three(values):
    high = values.astype(jnp.bfloat16)
    rest = values - high.astype(jnp.float32)
    middle = rest.astype(jnp.bfloat16)
    low = (rest - middle.astype(jnp.float32)).astype(jnp.bfloat16)
    return jnp.concatenate([high, middle, low], axis=0)


def index_plan(underlying_slot, chain_map, n_inst, myself, owner_rows, option_rows):
    f32 = jnp.float32
    count = underlying_slot.shape[0]
    high_count = -(-count // 128)
    table = jnp.pad(underlying_slot, (0, high_count * 128 - count)).reshape(high_count, 128)
    tables = jnp.concatenate([table // 64, table % 64], axis=1).astype(jnp.bfloat16)
    high = (chain_map // 128)[:, None] == jnp.arange(high_count, dtype=jnp.int32)[None, :]
    rows = jnp.dot(high.astype(jnp.bfloat16), tables, preferred_element_type=f32)
    rows = rows[:, :128] * 64.0 + rows[:, 128:]
    low = (chain_map % 128)[:, None] == jnp.arange(128, dtype=jnp.int32)[None, :]
    slots = jnp.sum(jnp.where(low, rows, 0.0), axis=1).astype(jnp.int32)
    slots = slots.reshape(n_inst, option_rows)
    blocks = chain_map.reshape(n_inst, option_rows)
    first = jnp.concatenate(
        [jnp.ones((n_inst, 1), bool), blocks[:, 1:] != blocks[:, :-1]], axis=1
    )
    owner = slots // owner_rows
    owners = jnp.arange(n_inst, dtype=jnp.int32)
    fresh = first[:, None, :] & (owner[:, None, :] == owners[None, :, None])
    parts = option_rows // 128
    upper = (jnp.arange(128)[:, None] <= jnp.arange(128)[None, :]).astype(jnp.bfloat16)
    inner = jnp.dot(
        fresh.astype(jnp.bfloat16).reshape(n_inst * n_inst * parts, 128),
        upper,
        preferred_element_type=f32,
    ).reshape(n_inst, n_inst, parts, 128)
    totals = inner[..., -1]
    before = jnp.arange(parts)[:, None] < jnp.arange(parts)[None, :]
    offsets = jnp.sum(jnp.where(before, totals[..., :, None], 0.0), axis=2)
    running = (inner + offsets[..., None]).reshape(n_inst, n_inst, option_rows)
    ranks = running.astype(jnp.int32) - 1
    own_rank = lax.dynamic_index_in_dim(ranks, myself, 1, keepdims=False)
    own_fresh = lax.dynamic_index_in_dim(fresh, myself, 1, keepdims=False)
    place = jnp.arange(CAP, dtype=jnp.int32)
    hit = (own_rank[:, None, :] == place[None, :, None]) & own_fresh[:, None, :]
    local = slots - myself * owner_rows + 1
    send_row = jnp.sum(jnp.where(hit, local[:, None, :], 0), axis=2) - 1
    my_rank = lax.dynamic_index_in_dim(ranks, myself, 0, keepdims=False)
    my_owner = lax.dynamic_index_in_dim(owner, myself, 0, keepdims=False)
    rank_here = jnp.sum(jnp.where(my_owner[None, :] == owners[:, None], my_rank, 0), axis=0)
    return send_row, my_owner * CAP + rank_here


def price_kernel(fr_ref, loads_ref, base_ref, expand_ref, params_ref, pos_ref, out_ref, held, pnl, lf_sc, rv_sc, f_sc, v_sc):
    options = expand_ref.shape[0]
    f32 = jnp.float32

    @pl.when(pl.program_id(0) == 0)
    def _():
        held[...] = (pos_ref[...].astype(f32) * contract_size).astype(jnp.bfloat16)

    loads = loads_ref[...]
    dims = (((1,), (1,)), ((), ()))
    shock_price = lax.dot_general(loads[:, :F], fr_ref[...], dims, preferred_element_type=f32)
    shock_vol = lax.dot_general(loads[:, F:], fr_ref[...], dims, preferred_element_type=f32)
    base = base_ref[...].astype(f32)
    forward = (base[:, 0:1] * jnp.exp(shock_price)).astype(jnp.bfloat16)
    vol = (base[:, 1:2] * jnp.exp(shock_vol)).astype(jnp.bfloat16)
    forward_wide = forward.astype(f32)
    vol_wide = vol.astype(f32)
    live = forward_wide > 0.0
    f_sc[...] = forward
    v_sc[...] = vol
    lf_sc[...] = split_three(jnp.log(jnp.where(live, forward_wide, 1.0)))
    rv_sc[...] = split_three(1.0 / jnp.where(live, vol_wide, 1.0))

    tile = 128

    def step(index, carry):
        rows = pl.ds(pl.multiple_of(index * tile, tile), tile)
        pick = expand_ref[rows, :]
        pick3 = jnp.concatenate([pick, pick, pick], axis=1)
        fwd = jnp.dot(pick, f_sc[...], preferred_element_type=f32)
        sig = jnp.dot(pick, v_sc[...], preferred_element_type=f32)
        log_f = jnp.dot(pick3, lf_sc[...], preferred_element_type=f32)
        inv_v = jnp.dot(pick3, rv_sc[...], preferred_element_type=f32)
        par = params_ref[rows, :]
        log_k, c1, c2 = par[:, 0:1], par[:, 1:2], par[:, 2:3]
        half_k, half_phi, v0 = par[:, 3:4], par[:, 4:5], par[:, 5:6]
        ratio = (log_f - log_k) * (inv_v * c1)
        half = sig * c2
        e1 = erf_points(ratio + half)
        e2 = erf_points(ratio - half)
        flat = par[:, 6:7]
        value = fwd * (half_phi + 0.5 * e1) - half_k * e2 - flat
        pnl[rows, :] = value.astype(jnp.bfloat16)
        return carry

    lax.fori_loop(0, options // tile, step, 0)
    out_ref[...] = jnp.dot(held[...], pnl[...], preferred_element_type=f32).astype(out_ref.dtype)


def body(
    factor_returns, betas, base_state, underlying_slot, chain_map, strike_index, expiry, positions
):
    n_inst = lax.axis_size("inst")
    myself = lax.axis_index("inst")
    owner_rows = betas.shape[0]
    option_rows = strike_index.shape[0]
    scen_cols = factor_returns.shape[0]
    accounts = positions.shape[0]
    f32 = jnp.float32
    send_row, lookup = index_plan(
        underlying_slot, chain_map, n_inst, myself, owner_rows, option_rows
    )
    select = (
        send_row.reshape(-1)[:, None] == jnp.arange(owner_rows, dtype=jnp.int32)[None, :]
    ).astype(jnp.bfloat16)
    send_loads = jnp.dot(select, betas, preferred_element_type=f32).astype(jnp.bfloat16)
    send_base = lax.dot_general(
        select, base_state, (((1,), (1,)), ((), ())), preferred_element_type=f32
    ).astype(jnp.bfloat16)
    send = jnp.concatenate([send_loads, jnp.pad(send_base, ((0, 0), (0, 126)))], axis=1)
    got = lax.all_to_all(
        send.reshape(n_inst, CAP, 256), "inst", split_axis=0, concat_axis=0, tiled=True
    ).reshape(n_inst * CAP, 256)
    loads = got[:, :128]
    base = got[:, 128:130]
    places = n_inst * CAP
    expand = lookup[:, None] == jnp.arange(places, dtype=jnp.int32)[None, :]
    expand = expand.astype(jnp.bfloat16)
    option_base = lax.dot_general(
        base, expand, (((0,), (1,)), ((), ())), preferred_element_type=f32
    )
    forward_zero, vol_zero = option_base[0], option_base[1]
    log_step = strike_step * strike_index.astype(f32)
    strike = forward_zero * jnp.exp(log_step)
    log_k = jnp.log(strike)
    root = jnp.sqrt(expiry)
    c1 = SQRT_HALF / root
    c2 = (0.5 * SQRT_HALF) * root
    half_phi = jnp.where(strike_index >= 0, 0.5, -0.5)
    ratio = -log_step / vol_zero * c1
    half = vol_zero * c2
    e1 = lax.erf(ratio + half)
    e2 = lax.erf(ratio - half)
    half_k = 0.5 * strike
    v0 = forward_zero * (half_phi + 0.5 * e1) - strike * (half_phi + 0.5 * e2)
    flat = v0 + half_phi * strike
    zero = jnp.zeros_like(v0)
    params = jnp.stack([log_k, c1, c2, half_k, half_phi, v0, flat, zero], axis=1)
    chunk = min(256, scen_cols)
    whole = pl.BlockSpec(memory_space=pltpu.VMEM)
    partial = pl.pallas_call(
        price_kernel,
        grid=(scen_cols // chunk,),
        out_shape=jax.ShapeDtypeStruct((accounts, scen_cols), jnp.bfloat16),
        in_specs=[pl.BlockSpec((chunk, F), lambda i: (i, 0)), whole, whole, whole, whole, whole],
        out_specs=pl.BlockSpec((accounts, chunk), lambda i: (0, i)),
        scratch_shapes=[
            pltpu.VMEM((accounts, option_rows), jnp.bfloat16),
            pltpu.VMEM((option_rows, chunk), jnp.bfloat16),
            pltpu.VMEM((3 * places, chunk), jnp.bfloat16),
            pltpu.VMEM((3 * places, chunk), jnp.bfloat16),
            pltpu.VMEM((places, chunk), jnp.bfloat16),
            pltpu.VMEM((places, chunk), jnp.bfloat16),
        ],
        compiler_params=pltpu.CompilerParams(vmem_limit_bytes=40 * 1024 * 1024),
    )(factor_returns, loads, base, expand, params, positions)
    losses = lax.psum_scatter(partial, "inst", scatter_dimension=0, tiled=True).astype(f32)
    margin = lax.pmax(jnp.max(losses, axis=1), "scen")
    return (losses, margin)


def solution(mesh):
    return jax.shard_map(
        body,
        mesh=mesh,
        in_specs=(
            P("scen", None),
            P("inst", None),
            P(None, "inst"),
            P(),
            P(),
            P("inst"),
            P("inst"),
            P(None, "inst"),
        ),
        out_specs=(P("inst", "scen"), P("inst")),
        check_vma=False,
    )
```

```python
import functools
import jax
import jax.numpy as jnp
from jax import lax
from jax.experimental import pallas as pl
from jax.experimental.pallas import tpu as pltpu
from jax.sharding import PartitionSpec as P

F = 64
CAP = 48
strike_step = 0.05
contract_size = 0.03125
ERF_Q = (1.1283797055307927, 0.10276548081347335, -0.0001843820436491351, -0.0006257211496349986, 8.971323300994763e-05, -5.9858035855426975e-06, 1.5896701753059672e-07)
SQRT_HALF = 0.7071067811865476


def erf_points(points):
    square = jnp.minimum(points * points, 16.0)
    poly = ERF_Q[-1]
    for coef in ERF_Q[-2::-1]:
        poly = poly * square + coef
    return jnp.tanh(points * poly)


def split_three(values):
    high = values.astype(jnp.bfloat16)
    rest = values - high.astype(jnp.float32)
    middle = rest.astype(jnp.bfloat16)
    low = (rest - middle.astype(jnp.float32)).astype(jnp.bfloat16)
    return jnp.concatenate([high, middle, low], axis=0)


def index_plan(underlying_slot, chain_map, n_inst, myself, owner_rows, option_rows):
    f32 = jnp.float32
    count = underlying_slot.shape[0]
    high_count = -(-count // 128)
    table = jnp.pad(underlying_slot, (0, high_count * 128 - count)).reshape(high_count, 128)
    tables = jnp.concatenate([table // 64, table % 64], axis=1).astype(jnp.bfloat16)
    high = (chain_map // 128)[:, None] == jnp.arange(high_count, dtype=jnp.int32)[None, :]
    rows = jnp.dot(high.astype(jnp.bfloat16), tables, preferred_element_type=f32)
    rows = rows[:, :128] * 64.0 + rows[:, 128:]
    low = (chain_map % 128)[:, None] == jnp.arange(128, dtype=jnp.int32)[None, :]
    slots = jnp.sum(jnp.where(low, rows, 0.0), axis=1).astype(jnp.int32)
    slots = slots.reshape(n_inst, option_rows)
    blocks = chain_map.reshape(n_inst, option_rows)
    first = jnp.concatenate(
        [jnp.ones((n_inst, 1), bool), blocks[:, 1:] != blocks[:, :-1]], axis=1
    )
    owner = slots // owner_rows
    owners = jnp.arange(n_inst, dtype=jnp.int32)
    fresh = first[:, None, :] & (owner[:, None, :] == owners[None, :, None])
    parts = option_rows // 128
    upper = (jnp.arange(128)[:, None] <= jnp.arange(128)[None, :]).astype(jnp.bfloat16)
    inner = jnp.dot(
        fresh.astype(jnp.bfloat16).reshape(n_inst * n_inst * parts, 128),
        upper,
        preferred_element_type=f32,
    ).reshape(n_inst, n_inst, parts, 128)
    totals = inner[..., -1]
    before = jnp.arange(parts)[:, None] < jnp.arange(parts)[None, :]
    offsets = jnp.sum(jnp.where(before, totals[..., :, None], 0.0), axis=2)
    running = (inner + offsets[..., None]).reshape(n_inst, n_inst, option_rows)
    ranks = running.astype(jnp.int32) - 1
    own_rank = lax.dynamic_index_in_dim(ranks, myself, 1, keepdims=False)
    own_fresh = lax.dynamic_index_in_dim(fresh, myself, 1, keepdims=False)
    place = jnp.arange(CAP, dtype=jnp.int32)
    hit = (own_rank[:, None, :] == place[None, :, None]) & own_fresh[:, None, :]
    local = slots - myself * owner_rows + 1
    send_row = jnp.sum(jnp.where(hit, local[:, None, :], 0), axis=2) - 1
    my_rank = lax.dynamic_index_in_dim(ranks, myself, 0, keepdims=False)
    my_owner = lax.dynamic_index_in_dim(owner, myself, 0, keepdims=False)
    rank_here = jnp.sum(jnp.where(my_owner[None, :] == owners[:, None], my_rank, 0), axis=0)
    return send_row, my_owner * CAP + rank_here


def price_kernel(fr_ref, loads_ref, base_ref, expand_ref, params_ref, pos_ref, out_ref, pnl, lf_sc, rv_sc, f_sc, v_sc):
    options = expand_ref.shape[0]
    f32 = jnp.float32

    loads = loads_ref[...]
    dims = (((1,), (1,)), ((), ()))
    shock_price = lax.dot_general(loads[:, :F], fr_ref[...], dims, preferred_element_type=f32)
    shock_vol = lax.dot_general(loads[:, F:], fr_ref[...], dims, preferred_element_type=f32)
    base = base_ref[...].astype(f32)
    forward = (base[:, 0:1] * jnp.exp(shock_price)).astype(jnp.bfloat16)
    vol = (base[:, 1:2] * jnp.exp(shock_vol)).astype(jnp.bfloat16)
    forward_wide = forward.astype(f32)
    vol_wide = vol.astype(f32)
    live = forward_wide > 0.0
    f_sc[...] = forward
    v_sc[...] = vol
    lf_sc[...] = split_three(jnp.log(jnp.where(live, forward_wide, 1.0)))
    rv_sc[...] = split_three(1.0 / jnp.where(live, vol_wide, 1.0))

    tile = 128

    def step(index, carry):
        rows = pl.ds(pl.multiple_of(index * tile, tile), tile)
        pick = expand_ref[rows, :]
        pick3 = jnp.concatenate([pick, pick, pick], axis=1)
        fwd = jnp.dot(pick, f_sc[...], preferred_element_type=f32)
        sig = jnp.dot(pick, v_sc[...], preferred_element_type=f32)
        log_f = jnp.dot(pick3, lf_sc[...], preferred_element_type=f32)
        inv_v = jnp.dot(pick3, rv_sc[...], preferred_element_type=f32)
        par = params_ref[rows, :]
        log_k, c1, c2 = par[:, 0:1], par[:, 1:2], par[:, 2:3]
        half_k, half_phi, v0 = par[:, 3:4], par[:, 4:5], par[:, 5:6]
        ratio = (log_f - log_k) * (inv_v * c1)
        half = sig * c2
        e1 = erf_points(ratio + half)
        e2 = erf_points(ratio - half)
        flat = par[:, 6:7]
        value = fwd * (half_phi + 0.5 * e1) - half_k * e2 - flat
        pnl[rows, :] = value.astype(jnp.bfloat16)
        return carry

    lax.fori_loop(0, options // tile, step, 0)
    out_ref[...] = jnp.dot(pos_ref[...], pnl[...], preferred_element_type=f32).astype(out_ref.dtype)


def body(
    factor_returns, betas, base_state, underlying_slot, chain_map, strike_index, expiry, positions
):
    n_inst = lax.axis_size("inst")
    myself = lax.axis_index("inst")
    owner_rows = betas.shape[0]
    option_rows = strike_index.shape[0]
    scen_cols = factor_returns.shape[0]
    accounts = positions.shape[0]
    f32 = jnp.float32
    send_row, lookup = index_plan(
        underlying_slot, chain_map, n_inst, myself, owner_rows, option_rows
    )
    select = (
        send_row.reshape(-1)[:, None] == jnp.arange(owner_rows, dtype=jnp.int32)[None, :]
    ).astype(jnp.bfloat16)
    send_loads = jnp.dot(select, betas, preferred_element_type=f32).astype(jnp.bfloat16)
    send_base = lax.dot_general(
        select, base_state, (((1,), (1,)), ((), ())), preferred_element_type=f32
    ).astype(jnp.bfloat16)
    send = jnp.concatenate([send_loads, jnp.pad(send_base, ((0, 0), (0, 126)))], axis=1)
    got = lax.all_to_all(
        send.reshape(n_inst, CAP, 256), "inst", split_axis=0, concat_axis=0, tiled=True
    ).reshape(n_inst * CAP, 256)
    loads = got[:, :128]
    base = got[:, 128:130]
    places = n_inst * CAP
    expand = lookup[:, None] == jnp.arange(places, dtype=jnp.int32)[None, :]
    expand = expand.astype(jnp.bfloat16)
    option_base = lax.dot_general(
        base, expand, (((0,), (1,)), ((), ())), preferred_element_type=f32
    )
    forward_zero, vol_zero = option_base[0], option_base[1]
    log_step = strike_step * strike_index.astype(f32)
    strike = forward_zero * jnp.exp(log_step)
    log_k = jnp.log(strike)
    root = jnp.sqrt(expiry)
    c1 = SQRT_HALF / root
    c2 = (0.5 * SQRT_HALF) * root
    half_phi = jnp.where(strike_index >= 0, 0.5, -0.5)
    ratio = -log_step / vol_zero * c1
    half = vol_zero * c2
    e1 = lax.erf(ratio + half)
    e2 = lax.erf(ratio - half)
    half_k = 0.5 * strike
    v0 = forward_zero * (half_phi + 0.5 * e1) - strike * (half_phi + 0.5 * e2)
    flat = v0 + half_phi * strike
    zero = jnp.zeros_like(v0)
    params = jnp.stack([log_k, c1, c2, half_k, half_phi, v0, flat, zero], axis=1)
    chunk = min(256, scen_cols)
    pieces = min(4, scen_cols // chunk)
    piece = scen_cols // pieces
    held = (contract_size * positions.astype(f32)).astype(jnp.bfloat16)
    whole = pl.BlockSpec(memory_space=pltpu.VMEM)
    price = pl.pallas_call(
        price_kernel,
        grid=(piece // chunk,),
        out_shape=jax.ShapeDtypeStruct((accounts, piece), jnp.bfloat16),
        in_specs=[pl.BlockSpec((chunk, F), lambda i: (i, 0)), whole, whole, whole, whole, whole],
        out_specs=pl.BlockSpec((accounts, chunk), lambda i: (0, i)),
        scratch_shapes=[
            pltpu.VMEM((option_rows, chunk), jnp.bfloat16),
            pltpu.VMEM((3 * places, chunk), jnp.bfloat16),
            pltpu.VMEM((3 * places, chunk), jnp.bfloat16),
            pltpu.VMEM((places, chunk), jnp.bfloat16),
            pltpu.VMEM((places, chunk), jnp.bfloat16),
        ],
        compiler_params=pltpu.CompilerParams(vmem_limit_bytes=24 * 1024 * 1024),
        cost_estimate=pl.CostEstimate(
            flops=60 * option_rows * piece * 64, bytes_accessed=8 << 20, transcendentals=0
        ),
    )
    sums = []
    for at in range(pieces):
        part = price(
            factor_returns[at * piece : (at + 1) * piece], loads, base, expand, params, held
        )
        sums.append(lax.psum_scatter(part, "inst", scatter_dimension=0, tiled=True))
    losses = jnp.concatenate(sums, axis=1).astype(f32)
    margin = lax.pmax(jnp.max(losses, axis=1), "scen")
    return (losses, margin)


def solution(mesh):
    return jax.shard_map(
        body,
        mesh=mesh,
        in_specs=(
            P("scen", None),
            P("inst", None),
            P(None, "inst"),
            P(),
            P(),
            P("inst"),
            P("inst"),
            P(None, "inst"),
        ),
        out_specs=(P("inst", "scen"), P("inst")),
        check_vma=False,
    )
```

```python
import functools
import jax
import jax.numpy as jnp
from jax import lax
from jax.experimental import pallas as pl
from jax.experimental.pallas import tpu as pltpu
from jax.sharding import PartitionSpec as P

F = 64
CAP = 48
strike_step = 0.05
contract_size = 0.03125
ERF_Q = (1.1283797055307927, 0.10276548081347335, -0.0001843820436491351, -0.0006257211496349986, 8.971323300994763e-05, -5.9858035855426975e-06, 1.5896701753059672e-07)
SQRT_HALF = 0.7071067811865476


def erf_points(points):
    square = jnp.minimum(points * points, 16.0)
    poly = ERF_Q[-1]
    for coef in ERF_Q[-2::-1]:
        poly = poly * square + coef
    return jnp.tanh(points * poly)


def split_three(values):
    high = values.astype(jnp.bfloat16)
    rest = values - high.astype(jnp.float32)
    middle = rest.astype(jnp.bfloat16)
    low = (rest - middle.astype(jnp.float32)).astype(jnp.bfloat16)
    return jnp.concatenate([high, middle, low], axis=0)


def index_plan(underlying_slot, chain_map, n_inst, myself, owner_rows, option_rows):
    f32 = jnp.float32
    count = underlying_slot.shape[0]
    high_count = -(-count // 128)
    table = jnp.pad(underlying_slot, (0, high_count * 128 - count)).reshape(high_count, 128)
    tables = jnp.concatenate([table // 64, table % 64], axis=1).astype(jnp.bfloat16)
    high = (chain_map // 128)[:, None] == jnp.arange(high_count, dtype=jnp.int32)[None, :]
    rows = jnp.dot(high.astype(jnp.bfloat16), tables, preferred_element_type=f32)
    rows = rows[:, :128] * 64.0 + rows[:, 128:]
    low = (chain_map % 128)[:, None] == jnp.arange(128, dtype=jnp.int32)[None, :]
    slots = jnp.sum(jnp.where(low, rows, 0.0), axis=1).astype(jnp.int32)
    slots = slots.reshape(n_inst, option_rows)
    blocks = chain_map.reshape(n_inst, option_rows)
    first = jnp.concatenate(
        [jnp.ones((n_inst, 1), bool), blocks[:, 1:] != blocks[:, :-1]], axis=1
    )
    owner = slots // owner_rows
    owners = jnp.arange(n_inst, dtype=jnp.int32)
    fresh = first[:, None, :] & (owner[:, None, :] == owners[None, :, None])
    parts = option_rows // 128
    upper = (jnp.arange(128)[:, None] <= jnp.arange(128)[None, :]).astype(jnp.bfloat16)
    inner = jnp.dot(
        fresh.astype(jnp.bfloat16).reshape(n_inst * n_inst * parts, 128),
        upper,
        preferred_element_type=f32,
    ).reshape(n_inst, n_inst, parts, 128)
    totals = inner[..., -1]
    before = jnp.arange(parts)[:, None] < jnp.arange(parts)[None, :]
    offsets = jnp.sum(jnp.where(before, totals[..., :, None], 0.0), axis=2)
    running = (inner + offsets[..., None]).reshape(n_inst, n_inst, option_rows)
    ranks = running.astype(jnp.int32) - 1
    own_rank = lax.dynamic_index_in_dim(ranks, myself, 1, keepdims=False)
    own_fresh = lax.dynamic_index_in_dim(fresh, myself, 1, keepdims=False)
    place = jnp.arange(CAP, dtype=jnp.int32)
    hit = (own_rank[:, None, :] == place[None, :, None]) & own_fresh[:, None, :]
    local = slots - myself * owner_rows + 1
    send_row = jnp.sum(jnp.where(hit, local[:, None, :], 0), axis=2) - 1
    my_rank = lax.dynamic_index_in_dim(ranks, myself, 0, keepdims=False)
    my_owner = lax.dynamic_index_in_dim(owner, myself, 0, keepdims=False)
    rank_here = jnp.sum(jnp.where(my_owner[None, :] == owners[:, None], my_rank, 0), axis=0)
    return send_row, my_owner * CAP + rank_here


def price_kernel(fr_ref, loads_ref, base_ref, expand_ref, params_ref, pos_ref, out_ref, pnl, lf_sc, rv_sc, f_sc, v_sc):
    options = expand_ref.shape[0]
    f32 = jnp.float32

    loads = loads_ref[...]
    dims = (((1,), (1,)), ((), ()))
    shock_price = lax.dot_general(loads[:, :F], fr_ref[...], dims, preferred_element_type=f32)
    shock_vol = lax.dot_general(loads[:, F:], fr_ref[...], dims, preferred_element_type=f32)
    base = base_ref[...].astype(f32)
    forward = (base[:, 0:1] * jnp.exp(shock_price)).astype(jnp.bfloat16)
    vol = (base[:, 1:2] * jnp.exp(shock_vol)).astype(jnp.bfloat16)
    forward_wide = forward.astype(f32)
    vol_wide = vol.astype(f32)
    live = forward_wide > 0.0
    f_sc[...] = forward
    v_sc[...] = vol
    lf_sc[...] = split_three(jnp.log(jnp.where(live, forward_wide, 1.0)))
    rv_sc[...] = split_three(1.0 / jnp.where(live, vol_wide, 1.0))

    tile = 128

    def step(index, carry):
        rows = pl.ds(pl.multiple_of(index * tile, tile), tile)
        pick = expand_ref[rows, :]
        pick3 = jnp.concatenate([pick, pick, pick], axis=1)
        fwd = jnp.dot(pick, f_sc[...], preferred_element_type=f32)
        sig = jnp.dot(pick, v_sc[...], preferred_element_type=f32)
        log_f = jnp.dot(pick3, lf_sc[...], preferred_element_type=f32)
        inv_v = jnp.dot(pick3, rv_sc[...], preferred_element_type=f32)
        par = params_ref[rows, :]
        log_k, c1, c2 = par[:, 0:1], par[:, 1:2], par[:, 2:3]
        half_k, half_phi, v0 = par[:, 3:4], par[:, 4:5], par[:, 5:6]
        ratio = (log_f - log_k) * (inv_v * c1)
        half = sig * c2
        e1 = erf_points(ratio + half)
        e2 = erf_points(ratio - half)
        flat = par[:, 6:7]
        value = fwd * (half_phi + 0.5 * e1) - half_k * e2 - flat
        pnl[rows, :] = value.astype(jnp.bfloat16)
        return carry

    lax.fori_loop(0, options // tile, step, 0)
    out_ref[...] = jnp.dot(pos_ref[...], pnl[...], preferred_element_type=f32).astype(out_ref.dtype)


def halving_sum(part, axis, myself, count):
    left = part.reshape(count, part.shape[0] // count, part.shape[1])
    bit = 1
    while bit < count:
        halves = left.reshape(left.shape[0] // 2, 2, left.shape[1], left.shape[2])
        mine = (myself // bit) % 2
        keep = lax.dynamic_index_in_dim(halves, mine, 1, keepdims=False)
        give = lax.dynamic_index_in_dim(halves, 1 - mine, 1, keepdims=False)
        pairs = [(i, i ^ bit) for i in range(count)]
        got = lax.ppermute(give.astype(jnp.bfloat16), axis, pairs)
        left = keep.astype(jnp.float32) + got.astype(jnp.float32)
        bit *= 2
    return left[0]


def body(
    factor_returns, betas, base_state, underlying_slot, chain_map, strike_index, expiry, positions
):
    n_inst = lax.axis_size("inst")
    myself = lax.axis_index("inst")
    owner_rows = betas.shape[0]
    option_rows = strike_index.shape[0]
    scen_cols = factor_returns.shape[0]
    accounts = positions.shape[0]
    f32 = jnp.float32
    send_row, lookup = index_plan(
        underlying_slot, chain_map, n_inst, myself, owner_rows, option_rows
    )
    select = (
        send_row.reshape(-1)[:, None] == jnp.arange(owner_rows, dtype=jnp.int32)[None, :]
    ).astype(jnp.bfloat16)
    send_loads = jnp.dot(select, betas, preferred_element_type=f32).astype(jnp.bfloat16)
    send_base = lax.dot_general(
        select, base_state, (((1,), (1,)), ((), ())), preferred_element_type=f32
    ).astype(jnp.bfloat16)
    send = jnp.concatenate([send_loads, jnp.pad(send_base, ((0, 0), (0, 126)))], axis=1)
    got = lax.all_to_all(
        send.reshape(n_inst, CAP, 256), "inst", split_axis=0, concat_axis=0, tiled=True
    ).reshape(n_inst * CAP, 256)
    loads = got[:, :128]
    base = got[:, 128:130]
    places = n_inst * CAP
    expand = lookup[:, None] == jnp.arange(places, dtype=jnp.int32)[None, :]
    expand = expand.astype(jnp.bfloat16)
    option_base = lax.dot_general(
        base, expand, (((0,), (1,)), ((), ())), preferred_element_type=f32
    )
    forward_zero, vol_zero = option_base[0], option_base[1]
    log_step = strike_step * strike_index.astype(f32)
    strike = forward_zero * jnp.exp(log_step)
    log_k = jnp.log(strike)
    root = jnp.sqrt(expiry)
    c1 = SQRT_HALF / root
    c2 = (0.5 * SQRT_HALF) * root
    half_phi = jnp.where(strike_index >= 0, 0.5, -0.5)
    ratio = -log_step / vol_zero * c1
    half = vol_zero * c2
    e1 = lax.erf(ratio + half)
    e2 = lax.erf(ratio - half)
    half_k = 0.5 * strike
    v0 = forward_zero * (half_phi + 0.5 * e1) - strike * (half_phi + 0.5 * e2)
    flat = v0 + half_phi * strike
    zero = jnp.zeros_like(v0)
    params = jnp.stack([log_k, c1, c2, half_k, half_phi, v0, flat, zero], axis=1)
    chunk = min(256, scen_cols)
    pieces = min(4, scen_cols // chunk)
    piece = scen_cols // pieces
    held = (contract_size * positions.astype(f32)).astype(jnp.bfloat16)
    whole = pl.BlockSpec(memory_space=pltpu.VMEM)
    price = pl.pallas_call(
        price_kernel,
        grid=(piece // chunk,),
        out_shape=jax.ShapeDtypeStruct((accounts, piece), jnp.bfloat16),
        in_specs=[pl.BlockSpec((chunk, F), lambda i: (i, 0)), whole, whole, whole, whole, whole],
        out_specs=pl.BlockSpec((accounts, chunk), lambda i: (0, i)),
        scratch_shapes=[
            pltpu.VMEM((option_rows, chunk), jnp.bfloat16),
            pltpu.VMEM((3 * places, chunk), jnp.bfloat16),
            pltpu.VMEM((3 * places, chunk), jnp.bfloat16),
            pltpu.VMEM((places, chunk), jnp.bfloat16),
            pltpu.VMEM((places, chunk), jnp.bfloat16),
        ],
        compiler_params=pltpu.CompilerParams(vmem_limit_bytes=24 * 1024 * 1024),
        cost_estimate=pl.CostEstimate(
            flops=60 * option_rows * piece * 64, bytes_accessed=8 << 20, transcendentals=0
        ),
    )
    sums = []
    for at in range(pieces):
        part = price(
            factor_returns[at * piece : (at + 1) * piece], loads, base, expand, params, held
        )
        sums.append(halving_sum(part, "inst", myself, n_inst))
    losses = jnp.concatenate(sums, axis=1)
    margin = functools.reduce(jnp.maximum, [jnp.max(one, axis=1) for one in sums])
    n_scen = lax.axis_size("scen")
    bit = 1
    while bit < n_scen:
        pairs = [(i, i ^ bit) for i in range(n_scen)]
        margin = jnp.maximum(margin, lax.ppermute(margin, "scen", pairs))
        bit *= 2
    return (losses, margin)


def solution(mesh):
    return jax.shard_map(
        body,
        mesh=mesh,
        in_specs=(
            P("scen", None),
            P("inst", None),
            P(None, "inst"),
            P(),
            P(),
            P("inst"),
            P("inst"),
            P(None, "inst"),
        ),
        out_specs=(P("inst", "scen"), P("inst")),
        check_vma=False,
    )
```

```python
import functools
import jax
import jax.numpy as jnp
from jax import lax
from jax.experimental import pallas as pl
from jax.experimental.pallas import tpu as pltpu
from jax.sharding import PartitionSpec as P

F = 64
CAP = 48
strike_step = 0.05
contract_size = 0.03125
ERF_Q = (1.1283797055307927, 0.10276548081347335, -0.0001843820436491351, -0.0006257211496349986, 8.971323300994763e-05, -5.9858035855426975e-06, 1.5896701753059672e-07)
SQRT_HALF = 0.7071067811865476


def erf_points(points):
    square = jnp.minimum(points * points, 16.0)
    poly = ERF_Q[-1]
    for coef in ERF_Q[-2::-1]:
        poly = poly * square + coef
    return jnp.tanh(points * poly)


def split_three(values):
    high = values.astype(jnp.bfloat16)
    rest = values - high.astype(jnp.float32)
    middle = rest.astype(jnp.bfloat16)
    low = (rest - middle.astype(jnp.float32)).astype(jnp.bfloat16)
    return jnp.concatenate([high, middle, low], axis=0)


def index_plan(underlying_slot, chain_map, n_inst, myself, owner_rows, option_rows):
    f32 = jnp.float32
    count = underlying_slot.shape[0]
    high_count = -(-count // 128)
    table = jnp.pad(underlying_slot, (0, high_count * 128 - count)).reshape(high_count, 128)
    tables = jnp.concatenate([table // 64, table % 64], axis=1).astype(jnp.bfloat16)
    high = (chain_map // 128)[:, None] == jnp.arange(high_count, dtype=jnp.int32)[None, :]
    rows = jnp.dot(high.astype(jnp.bfloat16), tables, preferred_element_type=f32)
    rows = rows[:, :128] * 64.0 + rows[:, 128:]
    low = (chain_map % 128)[:, None] == jnp.arange(128, dtype=jnp.int32)[None, :]
    slots = jnp.sum(jnp.where(low, rows, 0.0), axis=1).astype(jnp.int32)
    slots = slots.reshape(n_inst, option_rows)
    blocks = chain_map.reshape(n_inst, option_rows)
    first = jnp.concatenate(
        [jnp.ones((n_inst, 1), bool), blocks[:, 1:] != blocks[:, :-1]], axis=1
    )
    owner = slots // owner_rows
    owners = jnp.arange(n_inst, dtype=jnp.int32)
    fresh = first[:, None, :] & (owner[:, None, :] == owners[None, :, None])
    parts = option_rows // 128
    upper = (jnp.arange(128)[:, None] <= jnp.arange(128)[None, :]).astype(jnp.bfloat16)
    inner = jnp.dot(
        fresh.astype(jnp.bfloat16).reshape(n_inst * n_inst * parts, 128),
        upper,
        preferred_element_type=f32,
    ).reshape(n_inst, n_inst, parts, 128)
    totals = inner[..., -1]
    before = jnp.arange(parts)[:, None] < jnp.arange(parts)[None, :]
    offsets = jnp.sum(jnp.where(before, totals[..., :, None], 0.0), axis=2)
    running = (inner + offsets[..., None]).reshape(n_inst, n_inst, option_rows)
    ranks = running.astype(jnp.int32) - 1
    own_rank = lax.dynamic_index_in_dim(ranks, myself, 1, keepdims=False)
    own_fresh = lax.dynamic_index_in_dim(fresh, myself, 1, keepdims=False)
    place = jnp.arange(CAP, dtype=jnp.int32)
    hit = (own_rank[:, None, :] == place[None, :, None]) & own_fresh[:, None, :]
    local = slots - myself * owner_rows + 1
    send_row = jnp.sum(jnp.where(hit, local[:, None, :], 0), axis=2) - 1
    my_rank = lax.dynamic_index_in_dim(ranks, myself, 0, keepdims=False)
    my_owner = lax.dynamic_index_in_dim(owner, myself, 0, keepdims=False)
    rank_here = jnp.sum(jnp.where(my_owner[None, :] == owners[:, None], my_rank, 0), axis=0)
    return send_row, my_owner * CAP + rank_here


def price_kernel(n, stages, pieces, fr_ref, loads_ref, base_ref, expand_ref, params_ref, pos_ref, out_ref, pnl, lf_sc, rv_sc, f_sc, v_sc, part, send_sem, recv_sem, *buffers):
    recv, give, keep = buffers[:stages], buffers[stages : 2 * stages - 1], buffers[2 * stages - 1 :]
    piece = pl.program_id(0)
    me = lax.axis_index("inst")
    bits = [(me // (1 << s)) % 2 for s in range(stages)]
    partners = [me + (1 << s) * (1 - 2 * bits[s]) for s in range(stages)]
    rows_out, chunk = out_ref.shape[0], fr_ref.shape[0]

    @pl.when(piece == 0)
    def _():
        barrier = pltpu.get_barrier_semaphore()
        for partner in partners:
            pl.semaphore_signal(
                barrier, inc=1, device_id={"inst": partner}, device_id_type=pl.DeviceIdType.MESH
            )
        pl.semaphore_wait(barrier, stages)

    def copy(s, j):
        half = n >> (s + 1)
        if s == 0:
            source = part.at[j, pl.ds((1 - bits[0]) * half, half)]
        else:
            source = give[s - 1].at[j]
        return pltpu.make_async_remote_copy(
            src_ref=source,
            dst_ref=recv[s].at[j],
            send_sem=send_sem.at[s, j],
            recv_sem=recv_sem.at[s, j],
            device_id={"inst": partners[s]},
            device_id_type=pl.DeviceIdType.MESH,
        )

    def finish(s, j):
        copy(s, j).wait_recv()
        half = n >> (s + 1)

        def total(h):
            mine = part[j, bits[0] * half + h].astype(jnp.float32) if s == 0 else keep[s - 1][j, h]
            return mine + recv[s][j, h].astype(jnp.float32)

        if s == stages - 1:
            out_ref[:, pl.ds(pl.multiple_of(j * chunk, chunk), chunk)] = total(0)
            return
        quarter = half // 2
        for h in range(quarter):
            give[s][j, h] = total((1 - bits[s + 1]) * quarter + h).astype(jnp.bfloat16)
        copy(s + 1, j).start()
        for h in range(quarter):
            keep[s][j, h] = total(bits[s + 1] * quarter + h)

    options = expand_ref.shape[0]
    f32 = jnp.float32

    loads = loads_ref[...]
    dims = (((1,), (1,)), ((), ()))
    shock_price = lax.dot_general(loads[:, :F], fr_ref[...], dims, preferred_element_type=f32)
    shock_vol = lax.dot_general(loads[:, F:], fr_ref[...], dims, preferred_element_type=f32)
    base = base_ref[...].astype(f32)
    forward = (base[:, 0:1] * jnp.exp(shock_price)).astype(jnp.bfloat16)
    vol = (base[:, 1:2] * jnp.exp(shock_vol)).astype(jnp.bfloat16)
    forward_wide = forward.astype(f32)
    vol_wide = vol.astype(f32)
    live = forward_wide > 0.0
    f_sc[...] = forward
    v_sc[...] = vol
    lf_sc[...] = split_three(jnp.log(jnp.where(live, forward_wide, 1.0)))
    rv_sc[...] = split_three(1.0 / jnp.where(live, vol_wide, 1.0))

    tile = 128

    def step(index, carry):
        rows = pl.ds(pl.multiple_of(index * tile, tile), tile)
        pick = expand_ref[rows, :]
        pick3 = jnp.concatenate([pick, pick, pick], axis=1)
        fwd = jnp.dot(pick, f_sc[...], preferred_element_type=f32)
        sig = jnp.dot(pick, v_sc[...], preferred_element_type=f32)
        log_f = jnp.dot(pick3, lf_sc[...], preferred_element_type=f32)
        inv_v = jnp.dot(pick3, rv_sc[...], preferred_element_type=f32)
        par = params_ref[rows, :]
        log_k, c1, c2 = par[:, 0:1], par[:, 1:2], par[:, 2:3]
        half_k, half_phi, v0 = par[:, 3:4], par[:, 4:5], par[:, 5:6]
        ratio = (log_f - log_k) * (inv_v * c1)
        half = sig * c2
        e1 = erf_points(ratio + half)
        e2 = erf_points(ratio - half)
        flat = par[:, 6:7]
        value = fwd * (half_phi + 0.5 * e1) - half_k * e2 - flat
        pnl[rows, :] = value.astype(jnp.bfloat16)
        return carry

    lax.fori_loop(0, options // tile, step, 0)
    for block in range(n):
        place = sum(((block >> s) & 1) << (stages - 1 - s) for s in range(stages))
        part[piece, place] = jnp.dot(
            pos_ref[block * rows_out : (block + 1) * rows_out, :],
            pnl[...],
            preferred_element_type=f32,
        ).astype(jnp.bfloat16)
    copy(0, piece).start()
    for s in range(stages):
        @pl.when(piece > s)
        def _():
            finish(s, piece - 1 - s)

    @pl.when(piece == pieces - 1)
    def _():
        for s in range(stages):
            for j in range(max(0, pieces - 1 - s), pieces):
                finish(s, j)
        for s in range(stages):
            for j in range(pieces):
                copy(s, j).wait_send()


def body(
    factor_returns, betas, base_state, underlying_slot, chain_map, strike_index, expiry, positions
):
    n_inst = lax.axis_size("inst")
    myself = lax.axis_index("inst")
    owner_rows = betas.shape[0]
    option_rows = strike_index.shape[0]
    scen_cols = factor_returns.shape[0]
    accounts = positions.shape[0]
    f32 = jnp.float32
    send_row, lookup = index_plan(
        underlying_slot, chain_map, n_inst, myself, owner_rows, option_rows
    )
    select = (
        send_row.reshape(-1)[:, None] == jnp.arange(owner_rows, dtype=jnp.int32)[None, :]
    ).astype(jnp.bfloat16)
    send_loads = jnp.dot(select, betas, preferred_element_type=f32).astype(jnp.bfloat16)
    send_base = lax.dot_general(
        select, base_state, (((1,), (1,)), ((), ())), preferred_element_type=f32
    ).astype(jnp.bfloat16)
    send = jnp.concatenate([send_loads, jnp.pad(send_base, ((0, 0), (0, 126)))], axis=1)
    got = lax.all_to_all(
        send.reshape(n_inst, CAP, 256), "inst", split_axis=0, concat_axis=0, tiled=True
    ).reshape(n_inst * CAP, 256)
    loads = got[:, :128]
    base = got[:, 128:130]
    places = n_inst * CAP
    expand = lookup[:, None] == jnp.arange(places, dtype=jnp.int32)[None, :]
    expand = expand.astype(jnp.bfloat16)
    option_base = lax.dot_general(
        base, expand, (((0,), (1,)), ((), ())), preferred_element_type=f32
    )
    forward_zero, vol_zero = option_base[0], option_base[1]
    log_step = strike_step * strike_index.astype(f32)
    strike = forward_zero * jnp.exp(log_step)
    log_k = jnp.log(strike)
    root = jnp.sqrt(expiry)
    c1 = SQRT_HALF / root
    c2 = (0.5 * SQRT_HALF) * root
    half_phi = jnp.where(strike_index >= 0, 0.5, -0.5)
    ratio = -log_step / vol_zero * c1
    half = vol_zero * c2
    e1 = lax.erf(ratio + half)
    e2 = lax.erf(ratio - half)
    half_k = 0.5 * strike
    v0 = forward_zero * (half_phi + 0.5 * e1) - strike * (half_phi + 0.5 * e2)
    flat = v0 + half_phi * strike
    zero = jnp.zeros_like(v0)
    params = jnp.stack([log_k, c1, c2, half_k, half_phi, v0, flat, zero], axis=1)
    chunk = min(256, scen_cols)
    pieces = scen_cols // chunk
    stages = n_inst.bit_length() - 1
    rows = accounts // n_inst
    held = (contract_size * positions.astype(f32)).astype(jnp.bfloat16)
    whole = pl.BlockSpec(memory_space=pltpu.VMEM)
    sizes = [(pieces, n_inst >> (s + 1), rows, chunk) for s in range(stages)]
    losses = pl.pallas_call(
        functools.partial(price_kernel, n_inst, stages, pieces),
        grid=(pieces,),
        out_shape=jax.ShapeDtypeStruct((rows, scen_cols), f32),
        in_specs=[pl.BlockSpec((chunk, F), lambda i: (i, 0)), whole, whole, whole, whole, whole],
        out_specs=whole,
        scratch_shapes=[
            pltpu.VMEM((option_rows, chunk), jnp.bfloat16),
            pltpu.VMEM((3 * places, chunk), jnp.bfloat16),
            pltpu.VMEM((3 * places, chunk), jnp.bfloat16),
            pltpu.VMEM((places, chunk), jnp.bfloat16),
            pltpu.VMEM((places, chunk), jnp.bfloat16),
            pltpu.VMEM((pieces, n_inst, rows, chunk), jnp.bfloat16),
            pltpu.SemaphoreType.DMA((stages, pieces)),
            pltpu.SemaphoreType.DMA((stages, pieces)),
        ]
        + [pltpu.VMEM(size, jnp.bfloat16) for size in sizes]
        + [pltpu.VMEM(size, jnp.bfloat16) for size in sizes[1:]]
        + [pltpu.VMEM(size, f32) for size in sizes[1:]],
        compiler_params=pltpu.CompilerParams(
            vmem_limit_bytes=40 * 1024 * 1024, collective_id=0, has_side_effects=True
        ),
        cost_estimate=pl.CostEstimate(
            flops=60 * option_rows * scen_cols * 64, bytes_accessed=8 << 20, transcendentals=0
        ),
    )(factor_returns, loads, base, expand, params, held)
    margin = jnp.max(losses, axis=1)
    n_scen = lax.axis_size("scen")
    bit = 1
    while bit < n_scen:
        pairs = [(i, i ^ bit) for i in range(n_scen)]
        margin = jnp.maximum(margin, lax.ppermute(margin, "scen", pairs))
        bit *= 2
    return (losses, margin)


def solution(mesh):
    return jax.shard_map(
        body,
        mesh=mesh,
        in_specs=(
            P("scen", None),
            P("inst", None),
            P(None, "inst"),
            P(),
            P(),
            P("inst"),
            P("inst"),
            P(None, "inst"),
        ),
        out_specs=(P("inst", "scen"), P("inst")),
        check_vma=False,
    )
```

```python
import functools
import jax
import jax.numpy as jnp
from jax import lax
from jax.experimental import pallas as pl
from jax.experimental.pallas import tpu as pltpu
from jax.sharding import PartitionSpec as P

F = 64
CAP = 48
strike_step = 0.05
contract_size = 0.03125
ERF_Q = (1.1283797055307927, 0.10276548081347335, -0.0001843820436491351, -0.0006257211496349986, 8.971323300994763e-05, -5.9858035855426975e-06, 1.5896701753059672e-07)
SQRT_HALF = 0.7071067811865476


def erf_points(points):
    square = jnp.minimum(points * points, 16.0)
    poly = ERF_Q[-1]
    for coef in ERF_Q[-2::-1]:
        poly = poly * square + coef
    return jnp.tanh(points * poly)


def split_three(values):
    high = values.astype(jnp.bfloat16)
    rest = values - high.astype(jnp.float32)
    middle = rest.astype(jnp.bfloat16)
    low = (rest - middle.astype(jnp.float32)).astype(jnp.bfloat16)
    return jnp.concatenate([high, middle, low], axis=0)


def index_plan(underlying_slot, chain_map, n_inst, myself, owner_rows, option_rows):
    f32 = jnp.float32
    count = underlying_slot.shape[0]
    high_count = -(-count // 128)
    table = jnp.pad(underlying_slot, (0, high_count * 128 - count)).reshape(high_count, 128)
    tables = jnp.concatenate([table // 64, table % 64], axis=1).astype(jnp.bfloat16)
    high = (chain_map // 128)[:, None] == jnp.arange(high_count, dtype=jnp.int32)[None, :]
    rows = jnp.dot(high.astype(jnp.bfloat16), tables, preferred_element_type=f32)
    rows = rows[:, :128] * 64.0 + rows[:, 128:]
    low = (chain_map % 128)[:, None] == jnp.arange(128, dtype=jnp.int32)[None, :]
    slots = jnp.sum(jnp.where(low, rows, 0.0), axis=1).astype(jnp.int32)
    slots = slots.reshape(n_inst, option_rows)
    blocks = chain_map.reshape(n_inst, option_rows)
    first = jnp.concatenate(
        [jnp.ones((n_inst, 1), bool), blocks[:, 1:] != blocks[:, :-1]], axis=1
    )
    owner = slots // owner_rows
    owners = jnp.arange(n_inst, dtype=jnp.int32)
    fresh = first[:, None, :] & (owner[:, None, :] == owners[None, :, None])
    parts = option_rows // 128
    upper = (jnp.arange(128)[:, None] <= jnp.arange(128)[None, :]).astype(jnp.bfloat16)
    inner = jnp.dot(
        fresh.astype(jnp.bfloat16).reshape(n_inst * n_inst * parts, 128),
        upper,
        preferred_element_type=f32,
    ).reshape(n_inst, n_inst, parts, 128)
    totals = inner[..., -1]
    before = jnp.arange(parts)[:, None] < jnp.arange(parts)[None, :]
    offsets = jnp.sum(jnp.where(before, totals[..., :, None], 0.0), axis=2)
    running = (inner + offsets[..., None]).reshape(n_inst, n_inst, option_rows)
    ranks = running.astype(jnp.int32) - 1
    own_rank = lax.dynamic_index_in_dim(ranks, myself, 1, keepdims=False)
    own_fresh = lax.dynamic_index_in_dim(fresh, myself, 1, keepdims=False)
    place = jnp.arange(CAP, dtype=jnp.int32)
    hit = (own_rank[:, None, :] == place[None, :, None]) & own_fresh[:, None, :]
    local = slots - myself * owner_rows + 1
    send_row = jnp.sum(jnp.where(hit, local[:, None, :], 0), axis=2) - 1
    my_rank = lax.dynamic_index_in_dim(ranks, myself, 0, keepdims=False)
    my_owner = lax.dynamic_index_in_dim(owner, myself, 0, keepdims=False)
    rank_here = jnp.sum(jnp.where(my_owner[None, :] == owners[:, None], my_rank, 0), axis=0)
    return send_row, my_owner * CAP + rank_here


def swap_kernel(n, send_ref, pos_ref, got_ref, held_ref, landing, send_sem, recv_sem):
    me = lax.axis_index("inst")
    barrier = pltpu.get_barrier_semaphore()
    for d in range(1, n):
        pl.semaphore_signal(
            barrier,
            inc=1,
            device_id={"inst": (me + d) % n},
            device_id_type=pl.DeviceIdType.MESH,
        )
    pl.semaphore_wait(barrier, n - 1)
    copies = []
    for d in range(1, n):
        copies.append(
            pltpu.make_async_remote_copy(
                src_ref=send_ref.at[(me + d) % n],
                dst_ref=landing.at[d - 1],
                send_sem=send_sem.at[d - 1],
                recv_sem=recv_sem.at[d - 1],
                device_id={"inst": (me + d) % n},
                device_id_type=pl.DeviceIdType.MESH,
            )
        )
    for one in copies:
        one.start()
    got_ref[me] = send_ref[me]
    tile = 64

    def step(index, carry):
        rows = pl.ds(pl.multiple_of(index * tile, tile), tile)
        wide = pos_ref[rows, :].astype(jnp.float32) * contract_size
        held_ref[rows, :] = wide.astype(jnp.bfloat16)
        return carry

    lax.fori_loop(0, pos_ref.shape[0] // tile, step, 0)
    for d, one in enumerate(copies, 1):
        one.wait_recv()
        got_ref[(me + n - d) % n] = landing[d - 1]
    for one in copies:
        one.wait_send()


def price_kernel(n, stages, pieces, scen_stages, fr_ref, loads_ref, base_ref, expand_ref, params_ref, pos_ref, out_ref, top_ref, pnl, lf_sc, rv_sc, f_sc, v_sc, part, send_sem, recv_sem, best, beside, top_send, top_recv, *buffers):
    recv, give, keep = buffers[:stages], buffers[stages : 2 * stages - 1], buffers[2 * stages - 1 :]
    piece = pl.program_id(0)
    me = lax.axis_index("inst")
    bits = [(me // (1 << s)) % 2 for s in range(stages)]
    partners = [me + (1 << s) * (1 - 2 * bits[s]) for s in range(stages)]
    place_scen = lax.axis_index("scen")
    mates = [
        place_scen + (1 << s) * (1 - 2 * ((place_scen // (1 << s)) % 2)) for s in range(scen_stages)
    ]
    rows_out, chunk = out_ref.shape[0], fr_ref.shape[0]

    @pl.when(piece == 0)
    def _():
        barrier = pltpu.get_barrier_semaphore()
        for partner in partners:
            pl.semaphore_signal(
                barrier, inc=1, device_id={"inst": partner}, device_id_type=pl.DeviceIdType.MESH
            )
        for mate in mates:
            pl.semaphore_signal(
                barrier, inc=1, device_id={"scen": mate}, device_id_type=pl.DeviceIdType.MESH
            )
        pl.semaphore_wait(barrier, stages + scen_stages)

    def copy(s, j):
        half = n >> (s + 1)
        if s == 0:
            source = part.at[j, pl.ds((1 - bits[0]) * half, half)]
        else:
            source = give[s - 1].at[j]
        return pltpu.make_async_remote_copy(
            src_ref=source,
            dst_ref=recv[s].at[j],
            send_sem=send_sem.at[s, j],
            recv_sem=recv_sem.at[s, j],
            device_id={"inst": partners[s]},
            device_id_type=pl.DeviceIdType.MESH,
        )

    def finish(s, j):
        copy(s, j).wait_recv()
        half = n >> (s + 1)

        def total(h):
            mine = part[j, bits[0] * half + h].astype(jnp.float32) if s == 0 else keep[s - 1][j, h]
            return mine + recv[s][j, h].astype(jnp.float32)

        if s == stages - 1:
            out_ref[:, pl.ds(pl.multiple_of(j * chunk, chunk), chunk)] = total(0)
            return
        quarter = half // 2
        for h in range(quarter):
            give[s][j, h] = total((1 - bits[s + 1]) * quarter + h).astype(jnp.bfloat16)
        copy(s + 1, j).start()
        for h in range(quarter):
            keep[s][j, h] = total(bits[s + 1] * quarter + h)

    options = expand_ref.shape[0]
    f32 = jnp.float32

    loads = loads_ref[...]
    dims = (((1,), (1,)), ((), ()))
    shock_price = lax.dot_general(loads[:, :F], fr_ref[...], dims, preferred_element_type=f32)
    shock_vol = lax.dot_general(loads[:, F:], fr_ref[...], dims, preferred_element_type=f32)
    base = base_ref[...].astype(f32)
    forward = (base[:, 0:1] * jnp.exp(shock_price)).astype(jnp.bfloat16)
    vol = (base[:, 1:2] * jnp.exp(shock_vol)).astype(jnp.bfloat16)
    forward_wide = forward.astype(f32)
    vol_wide = vol.astype(f32)
    live = forward_wide > 0.0
    f_sc[...] = forward
    v_sc[...] = vol
    lf_sc[...] = split_three(jnp.log(jnp.where(live, forward_wide, 1.0)))
    rv_sc[...] = split_three(1.0 / jnp.where(live, vol_wide, 1.0))

    tile = 128

    def step(index, carry):
        rows = pl.ds(pl.multiple_of(index * tile, tile), tile)
        pick = expand_ref[rows, :]
        pick3 = jnp.concatenate([pick, pick, pick], axis=1)
        fwd = jnp.dot(pick, f_sc[...], preferred_element_type=f32)
        sig = jnp.dot(pick, v_sc[...], preferred_element_type=f32)
        log_f = jnp.dot(pick3, lf_sc[...], preferred_element_type=f32)
        inv_v = jnp.dot(pick3, rv_sc[...], preferred_element_type=f32)
        par = params_ref[rows, :]
        log_k, c1, c2 = par[:, 0:1], par[:, 1:2], par[:, 2:3]
        half_k, half_phi, v0 = par[:, 3:4], par[:, 4:5], par[:, 5:6]
        ratio = (log_f - log_k) * (inv_v * c1)
        half = sig * c2
        e1 = erf_points(ratio + half)
        e2 = erf_points(ratio - half)
        flat = par[:, 6:7]
        value = fwd * (half_phi + 0.5 * e1) - half_k * e2 - flat
        pnl[rows, :] = value.astype(jnp.bfloat16)
        return carry

    lax.fori_loop(0, options // tile, step, 0)
    for block in range(n):
        place = sum(((block >> s) & 1) << (stages - 1 - s) for s in range(stages))
        part[piece, place] = jnp.dot(
            pos_ref[block * rows_out : (block + 1) * rows_out, :],
            pnl[...],
            preferred_element_type=f32,
        ).astype(jnp.bfloat16)
    copy(0, piece).start()
    for s in range(stages):
        @pl.when(piece > s)
        def _():
            finish(s, piece - 1 - s)

    @pl.when(piece == pieces - 1)
    def _():
        for s in range(stages):
            for j in range(max(0, pieces - 1 - s), pieces):
                finish(s, j)
        top = out_ref[:, 0:128]
        for at in range(128, out_ref.shape[1], 128):
            top = jnp.maximum(top, out_ref[:, at : at + 128])
        top = jnp.max(top.T, axis=0, keepdims=True)
        best[0] = jnp.broadcast_to(top, best.shape[1:])
        hops = []
        for s in range(scen_stages):
            hop = pltpu.make_async_remote_copy(
                src_ref=best.at[s],
                dst_ref=beside.at[s],
                send_sem=top_send.at[s],
                recv_sem=top_recv.at[s],
                device_id={"scen": mates[s]},
                device_id_type=pl.DeviceIdType.MESH,
            )
            hop.start()
            hop.wait_recv()
            best[s + 1] = jnp.maximum(best[s], beside[s])
            hops.append(hop)
        top_ref[...] = best[scen_stages]
        for hop in hops:
            hop.wait_send()
        for s in range(stages):
            for j in range(pieces):
                copy(s, j).wait_send()


def body(
    factor_returns, betas, base_state, underlying_slot, chain_map, strike_index, expiry, positions
):
    n_inst = lax.axis_size("inst")
    myself = lax.axis_index("inst")
    owner_rows = betas.shape[0]
    option_rows = strike_index.shape[0]
    scen_cols = factor_returns.shape[0]
    accounts = positions.shape[0]
    f32 = jnp.float32
    send_row, lookup = index_plan(
        underlying_slot, chain_map, n_inst, myself, owner_rows, option_rows
    )
    select = (
        send_row.reshape(-1)[:, None] == jnp.arange(owner_rows, dtype=jnp.int32)[None, :]
    ).astype(jnp.bfloat16)
    send_loads = jnp.dot(select, betas, preferred_element_type=f32).astype(jnp.bfloat16)
    send_base = lax.dot_general(
        select, base_state, (((1,), (1,)), ((), ())), preferred_element_type=f32
    ).astype(jnp.bfloat16)
    send = jnp.concatenate([send_loads, jnp.pad(send_base, ((0, 0), (0, 126)))], axis=1)
    whole = pl.BlockSpec(memory_space=pltpu.VMEM)
    got, held = pl.pallas_call(
        functools.partial(swap_kernel, n_inst),
        out_shape=(
            jax.ShapeDtypeStruct((n_inst, CAP, 256), jnp.bfloat16),
            jax.ShapeDtypeStruct((accounts, option_rows), jnp.bfloat16),
        ),
        in_specs=[whole, whole],
        out_specs=(whole, whole),
        scratch_shapes=[
            pltpu.VMEM((n_inst - 1, CAP, 256), jnp.bfloat16),
            pltpu.SemaphoreType.DMA((n_inst - 1,)),
            pltpu.SemaphoreType.DMA((n_inst - 1,)),
        ],
        compiler_params=pltpu.CompilerParams(
            vmem_limit_bytes=16 * 1024 * 1024, collective_id=1, has_side_effects=True
        ),
    )(send.reshape(n_inst, CAP, 256), positions)
    got = got.reshape(n_inst * CAP, 256)
    loads = got[:, :128]
    base = got[:, 128:130]
    places = n_inst * CAP
    expand = lookup[:, None] == jnp.arange(places, dtype=jnp.int32)[None, :]
    expand = expand.astype(jnp.bfloat16)
    option_base = lax.dot_general(
        base, expand, (((0,), (1,)), ((), ())), preferred_element_type=f32
    )
    forward_zero, vol_zero = option_base[0], option_base[1]
    log_step = strike_step * strike_index.astype(f32)
    strike = forward_zero * jnp.exp(log_step)
    log_k = jnp.log(strike)
    root = jnp.sqrt(expiry)
    c1 = SQRT_HALF / root
    c2 = (0.5 * SQRT_HALF) * root
    half_phi = jnp.where(strike_index >= 0, 0.5, -0.5)
    ratio = -log_step / vol_zero * c1
    half = vol_zero * c2
    e1 = lax.erf(ratio + half)
    e2 = lax.erf(ratio - half)
    half_k = 0.5 * strike
    v0 = forward_zero * (half_phi + 0.5 * e1) - strike * (half_phi + 0.5 * e2)
    flat = v0 + half_phi * strike
    zero = jnp.zeros_like(v0)
    params = jnp.stack([log_k, c1, c2, half_k, half_phi, v0, flat, zero], axis=1)
    chunk = min(256, scen_cols)
    pieces = scen_cols // chunk
    stages = n_inst.bit_length() - 1
    rows = accounts // n_inst
    scen_stages = lax.axis_size("scen").bit_length() - 1
    sizes = [(pieces, n_inst >> (s + 1), rows, chunk) for s in range(stages)]
    losses, top = pl.pallas_call(
        functools.partial(price_kernel, n_inst, stages, pieces, scen_stages),
        grid=(pieces,),
        out_shape=(
            jax.ShapeDtypeStruct((rows, scen_cols), f32),
            jax.ShapeDtypeStruct((8, rows), f32),
        ),
        in_specs=[pl.BlockSpec((chunk, F), lambda i: (i, 0)), whole, whole, whole, whole, whole],
        out_specs=(whole, whole),
        scratch_shapes=[
            pltpu.VMEM((option_rows, chunk), jnp.bfloat16),
            pltpu.VMEM((3 * places, chunk), jnp.bfloat16),
            pltpu.VMEM((3 * places, chunk), jnp.bfloat16),
            pltpu.VMEM((places, chunk), jnp.bfloat16),
            pltpu.VMEM((places, chunk), jnp.bfloat16),
            pltpu.VMEM((pieces, n_inst, rows, chunk), jnp.bfloat16),
            pltpu.SemaphoreType.DMA((stages, pieces)),
            pltpu.SemaphoreType.DMA((stages, pieces)),
            pltpu.VMEM((scen_stages + 1, 8, rows), f32),
            pltpu.VMEM((scen_stages, 8, rows), f32),
            pltpu.SemaphoreType.DMA((scen_stages,)),
            pltpu.SemaphoreType.DMA((scen_stages,)),
        ]
        + [pltpu.VMEM(size, jnp.bfloat16) for size in sizes]
        + [pltpu.VMEM(size, jnp.bfloat16) for size in sizes[1:]]
        + [pltpu.VMEM(size, f32) for size in sizes[1:]],
        compiler_params=pltpu.CompilerParams(
            vmem_limit_bytes=24 * 1024 * 1024, collective_id=0, has_side_effects=True
        ),
        cost_estimate=pl.CostEstimate(
            flops=60 * option_rows * scen_cols * 64, bytes_accessed=8 << 20, transcendentals=0
        ),
    )(factor_returns, loads, base, expand, params, held)
    margin = top[0]
    return (losses, margin)


def solution(mesh):
    return jax.shard_map(
        body,
        mesh=mesh,
        in_specs=(
            P("scen", None),
            P("inst", None),
            P(None, "inst"),
            P(),
            P(),
            P("inst"),
            P("inst"),
            P(None, "inst"),
        ),
        out_specs=(P("inst", "scen"), P("inst")),
        check_vma=False,
    )
```

```python
import functools
import jax
import jax.numpy as jnp
from jax import lax
from jax.experimental import pallas as pl
from jax.experimental.pallas import tpu as pltpu
from jax.sharding import PartitionSpec as P

F = 64
CAP = 48
strike_step = 0.05
contract_size = 0.03125
ERF_Q = (1.1283797055307927, 0.10276548081347335, -0.0001843820436491351, -0.0006257211496349986, 8.971323300994763e-05, -5.9858035855426975e-06, 1.5896701753059672e-07)
SQRT_HALF = 0.7071067811865476


def erf_points(points):
    square = jnp.minimum(points * points, 16.0)
    poly = ERF_Q[-1]
    for coef in ERF_Q[-2::-1]:
        poly = poly * square + coef
    return jnp.tanh(points * poly)


def split_three(values):
    high = values.astype(jnp.bfloat16)
    rest = values - high.astype(jnp.float32)
    middle = rest.astype(jnp.bfloat16)
    low = (rest - middle.astype(jnp.float32)).astype(jnp.bfloat16)
    return jnp.concatenate([high, middle, low], axis=0)


def index_plan(underlying_slot, chain_map, n_inst, myself, owner_rows, option_rows):
    f32 = jnp.float32
    count = underlying_slot.shape[0]
    high_count = -(-count // 128)
    table = jnp.pad(underlying_slot, (0, high_count * 128 - count)).reshape(high_count, 128)
    tables = jnp.concatenate([table // 64, table % 64], axis=1).astype(jnp.bfloat16)
    high = (chain_map // 128)[:, None] == jnp.arange(high_count, dtype=jnp.int32)[None, :]
    rows = jnp.dot(high.astype(jnp.bfloat16), tables, preferred_element_type=f32)
    rows = rows[:, :128] * 64.0 + rows[:, 128:]
    low = (chain_map % 128)[:, None] == jnp.arange(128, dtype=jnp.int32)[None, :]
    slots = jnp.sum(jnp.where(low, rows, 0.0), axis=1).astype(jnp.int32)
    slots = slots.reshape(n_inst, option_rows)
    blocks = chain_map.reshape(n_inst, option_rows)
    first = jnp.concatenate(
        [jnp.ones((n_inst, 1), bool), blocks[:, 1:] != blocks[:, :-1]], axis=1
    )
    owner = slots // owner_rows
    owners = jnp.arange(n_inst, dtype=jnp.int32)
    fresh = first[:, None, :] & (owner[:, None, :] == owners[None, :, None])
    parts = option_rows // 128
    upper = (jnp.arange(128)[:, None] <= jnp.arange(128)[None, :]).astype(jnp.bfloat16)
    inner = jnp.dot(
        fresh.astype(jnp.bfloat16).reshape(n_inst * n_inst * parts, 128),
        upper,
        preferred_element_type=f32,
    ).reshape(n_inst, n_inst, parts, 128)
    totals = inner[..., -1]
    before = jnp.arange(parts)[:, None] < jnp.arange(parts)[None, :]
    offsets = jnp.sum(jnp.where(before, totals[..., :, None], 0.0), axis=2)
    running = (inner + offsets[..., None]).reshape(n_inst, n_inst, option_rows)
    ranks = running.astype(jnp.int32) - 1
    own_rank = lax.dynamic_index_in_dim(ranks, myself, 1, keepdims=False)
    own_fresh = lax.dynamic_index_in_dim(fresh, myself, 1, keepdims=False)
    place = jnp.arange(CAP, dtype=jnp.int32)
    hit = (own_rank[:, None, :] == place[None, :, None]) & own_fresh[:, None, :]
    local = slots - myself * owner_rows + 1
    send_row = jnp.sum(jnp.where(hit, local[:, None, :], 0), axis=2) - 1
    my_rank = lax.dynamic_index_in_dim(ranks, myself, 0, keepdims=False)
    my_owner = lax.dynamic_index_in_dim(owner, myself, 0, keepdims=False)
    rank_here = jnp.sum(jnp.where(my_owner[None, :] == owners[:, None], my_rank, 0), axis=0)
    return send_row, my_owner * CAP + rank_here


def swap_kernel(n, send_ref, pos_ref, got_ref, held_ref, landing, send_sem, recv_sem):
    me = lax.axis_index("inst")
    barrier = pltpu.get_barrier_semaphore()
    for d in range(1, n):
        pl.semaphore_signal(
            barrier,
            inc=1,
            device_id={"inst": (me + d) % n},
            device_id_type=pl.DeviceIdType.MESH,
        )
    pl.semaphore_wait(barrier, n - 1)
    copies = []
    for d in range(1, n):
        copies.append(
            pltpu.make_async_remote_copy(
                src_ref=send_ref.at[(me + d) % n],
                dst_ref=landing.at[d - 1],
                send_sem=send_sem.at[d - 1],
                recv_sem=recv_sem.at[d - 1],
                device_id={"inst": (me + d) % n},
                device_id_type=pl.DeviceIdType.MESH,
            )
        )
    for one in copies:
        one.start()
    got_ref[me] = send_ref[me]
    tile = 64

    def step(index, carry):
        rows = pl.ds(pl.multiple_of(index * tile, tile), tile)
        wide = pos_ref[rows, :].astype(jnp.float32) * contract_size
        held_ref[rows, :] = wide.astype(jnp.bfloat16)
        return carry

    lax.fori_loop(0, pos_ref.shape[0] // tile, step, 0)
    for d, one in enumerate(copies, 1):
        one.wait_recv()
        got_ref[(me + n - d) % n] = landing[d - 1]
    for one in copies:
        one.wait_send()


def price_kernel(n, stages, pieces, scen_stages, fr_ref, loads_ref, base_ref, expand_ref, params_ref, pos_ref, out_ref, top_ref, pnl, lf_sc, rv_sc, f_sc, v_sc, part, send_sem, recv_sem, best, beside, top_send, top_recv, *buffers):
    recv, give, keep = buffers[:stages], buffers[stages : 2 * stages - 1], buffers[2 * stages - 1 :]
    piece = pl.program_id(0)
    me = lax.axis_index("inst")
    bits = [(me // (1 << s)) % 2 for s in range(stages)]
    partners = [me + (1 << s) * (1 - 2 * bits[s]) for s in range(stages)]
    place_scen = lax.axis_index("scen")
    mates = [
        place_scen + (1 << s) * (1 - 2 * ((place_scen // (1 << s)) % 2)) for s in range(scen_stages)
    ]
    rows_out, chunk = out_ref.shape[0], fr_ref.shape[0]

    @pl.when(piece == 0)
    def _():
        barrier = pltpu.get_barrier_semaphore()
        for partner in partners:
            pl.semaphore_signal(
                barrier, inc=1, device_id={"inst": partner}, device_id_type=pl.DeviceIdType.MESH
            )
        for mate in mates:
            pl.semaphore_signal(
                barrier, inc=1, device_id={"scen": mate}, device_id_type=pl.DeviceIdType.MESH
            )
        pl.semaphore_wait(barrier, stages + scen_stages)

    def copy(s, j):
        half = n >> (s + 1)
        if s == 0:
            source = part.at[j, pl.ds((1 - bits[0]) * half, half)]
        else:
            source = give[s - 1].at[j]
        return pltpu.make_async_remote_copy(
            src_ref=source,
            dst_ref=recv[s].at[j],
            send_sem=send_sem.at[s, j],
            recv_sem=recv_sem.at[s, j],
            device_id={"inst": partners[s]},
            device_id_type=pl.DeviceIdType.MESH,
        )

    def finish(s, j):
        copy(s, j).wait_recv()
        half = n >> (s + 1)

        def total(h):
            mine = part[j, bits[0] * half + h].astype(jnp.float32) if s == 0 else keep[s - 1][j, h]
            return mine + recv[s][j, h].astype(jnp.float32)

        if s == stages - 1:
            out_ref[:, pl.ds(pl.multiple_of(j * chunk, chunk), chunk)] = total(0)
            return
        quarter = half // 2
        for h in range(quarter):
            give[s][j, h] = total((1 - bits[s + 1]) * quarter + h).astype(jnp.bfloat16)
        copy(s + 1, j).start()
        for h in range(quarter):
            keep[s][j, h] = total(bits[s + 1] * quarter + h)

    options = expand_ref.shape[0]
    f32 = jnp.float32

    loads = loads_ref[...]
    dims = (((1,), (1,)), ((), ()))
    shock_price = lax.dot_general(loads[:, :F], fr_ref[...], dims, preferred_element_type=f32)
    shock_vol = lax.dot_general(loads[:, F:], fr_ref[...], dims, preferred_element_type=f32)
    base = base_ref[...].astype(f32)
    forward = (base[:, 0:1] * jnp.exp(shock_price)).astype(jnp.bfloat16)
    vol = (base[:, 1:2] * jnp.exp(shock_vol)).astype(jnp.bfloat16)
    forward_wide = forward.astype(f32)
    vol_wide = vol.astype(f32)
    live = forward_wide > 0.0
    f_sc[...] = forward
    v_sc[...] = vol
    lf_sc[...] = split_three(jnp.log(jnp.where(live, forward_wide, 1.0)))
    rv_sc[...] = split_three(1.0 / jnp.where(live, vol_wide, 1.0))

    tile = 128

    def step(index, carry):
        rows = pl.ds(pl.multiple_of(index * tile, tile), tile)
        pick = expand_ref[rows, :]
        pick3 = jnp.concatenate([pick, pick, pick], axis=1)
        fwd = jnp.dot(pick, f_sc[...], preferred_element_type=f32)
        sig = jnp.dot(pick, v_sc[...], preferred_element_type=f32)
        log_f = jnp.dot(pick3, lf_sc[...], preferred_element_type=f32)
        inv_v = jnp.dot(pick3, rv_sc[...], preferred_element_type=f32)
        par = params_ref[rows, :]
        log_k, c1, c2 = par[:, 0:1], par[:, 1:2], par[:, 2:3]
        half_k, half_phi, v0 = par[:, 3:4], par[:, 4:5], par[:, 5:6]
        ratio = (log_f - log_k) * (inv_v * c1)
        half = sig * c2
        e1 = erf_points(ratio + half)
        e2 = erf_points(ratio - half)
        flat = par[:, 6:7]
        value = fwd * (half_phi + 0.5 * e1) - half_k * e2 - flat
        pnl[rows, :] = value.astype(jnp.bfloat16)
        return carry

    lax.fori_loop(0, options // tile, step, 0)
    for block in range(n):
        place = sum(((block >> s) & 1) << (stages - 1 - s) for s in range(stages))
        part[piece, place] = jnp.dot(
            pos_ref[block * rows_out : (block + 1) * rows_out, :],
            pnl[...],
            preferred_element_type=f32,
        ).astype(jnp.bfloat16)
    copy(0, piece).start()
    for s in range(stages):
        @pl.when(piece > s)
        def _():
            finish(s, piece - 1 - s)

    @pl.when(piece == pieces - 1)
    def _():
        for s in range(stages):
            for j in range(max(0, pieces - 1 - s), pieces):
                finish(s, j)
        top = out_ref[:, 0:128]
        for at in range(128, out_ref.shape[1], 128):
            top = jnp.maximum(top, out_ref[:, at : at + 128])
        top = jnp.max(top.T, axis=0, keepdims=True)
        best[0] = jnp.broadcast_to(top, best.shape[1:])
        hops = []
        for s in range(scen_stages):
            hop = pltpu.make_async_remote_copy(
                src_ref=best.at[s],
                dst_ref=beside.at[s],
                send_sem=top_send.at[s],
                recv_sem=top_recv.at[s],
                device_id={"scen": mates[s]},
                device_id_type=pl.DeviceIdType.MESH,
            )
            hop.start()
            hop.wait_recv()
            best[s + 1] = jnp.maximum(best[s], beside[s])
            hops.append(hop)
        top_ref[...] = best[scen_stages]
        for hop in hops:
            hop.wait_send()
        for s in range(stages):
            for j in range(pieces):
                copy(s, j).wait_send()


def body(
    factor_returns, betas, base_state, underlying_slot, chain_map, strike_index, expiry, positions
):
    n_inst = lax.axis_size("inst")
    myself = lax.axis_index("inst")
    owner_rows = betas.shape[0]
    option_rows = strike_index.shape[0]
    scen_cols = factor_returns.shape[0]
    accounts = positions.shape[0]
    f32 = jnp.float32
    send_row, lookup = index_plan(
        underlying_slot, chain_map, n_inst, myself, owner_rows, option_rows
    )
    select = (
        send_row.reshape(-1)[:, None] == jnp.arange(owner_rows, dtype=jnp.int32)[None, :]
    ).astype(jnp.bfloat16)
    send_loads = jnp.dot(select, betas, preferred_element_type=f32).astype(jnp.bfloat16)
    send_base = lax.dot_general(
        select, base_state, (((1,), (1,)), ((), ())), preferred_element_type=f32
    ).astype(jnp.bfloat16)
    send = jnp.concatenate([send_loads, jnp.pad(send_base, ((0, 0), (0, 126)))], axis=1)
    whole = pl.BlockSpec(memory_space=pltpu.VMEM)
    got, held = pl.pallas_call(
        functools.partial(swap_kernel, n_inst),
        out_shape=(
            jax.ShapeDtypeStruct((n_inst, CAP, 256), jnp.bfloat16),
            jax.ShapeDtypeStruct((accounts, option_rows), jnp.bfloat16),
        ),
        in_specs=[whole, whole],
        out_specs=(whole, whole),
        scratch_shapes=[
            pltpu.VMEM((n_inst - 1, CAP, 256), jnp.bfloat16),
            pltpu.SemaphoreType.DMA((n_inst - 1,)),
            pltpu.SemaphoreType.DMA((n_inst - 1,)),
        ],
        compiler_params=pltpu.CompilerParams(
            vmem_limit_bytes=16 * 1024 * 1024, collective_id=1, has_side_effects=True
        ),
    )(send.reshape(n_inst, CAP, 256), positions)
    got = got.reshape(n_inst * CAP, 256)
    loads = got[:, :128]
    base = got[:, 128:130]
    places = n_inst * CAP
    expand = lookup[:, None] == jnp.arange(places, dtype=jnp.int32)[None, :]
    expand = expand.astype(jnp.bfloat16)
    option_base = lax.dot_general(
        base, expand, (((0,), (1,)), ((), ())), preferred_element_type=f32
    )
    forward_zero, vol_zero = option_base[0], option_base[1]
    log_step = strike_step * strike_index.astype(f32)
    strike = forward_zero * jnp.exp(log_step)
    log_k = jnp.log(strike)
    root = jnp.sqrt(expiry)
    c1 = SQRT_HALF / root
    c2 = (0.5 * SQRT_HALF) * root
    half_phi = jnp.where(strike_index >= 0, 0.5, -0.5)
    ratio = -log_step / vol_zero * c1
    half = vol_zero * c2
    e1 = lax.erf(ratio + half)
    e2 = lax.erf(ratio - half)
    half_k = 0.5 * strike
    v0 = forward_zero * (half_phi + 0.5 * e1) - strike * (half_phi + 0.5 * e2)
    flat = v0 + half_phi * strike
    zero = jnp.zeros_like(v0)
    params = jnp.stack([log_k, c1, c2, half_k, half_phi, v0, flat, zero], axis=1)
    chunk = min(128, scen_cols)
    pieces = scen_cols // chunk
    stages = n_inst.bit_length() - 1
    rows = accounts // n_inst
    scen_stages = lax.axis_size("scen").bit_length() - 1
    sizes = [(pieces, n_inst >> (s + 1), rows, chunk) for s in range(stages)]
    losses, top = pl.pallas_call(
        functools.partial(price_kernel, n_inst, stages, pieces, scen_stages),
        grid=(pieces,),
        out_shape=(
            jax.ShapeDtypeStruct((rows, scen_cols), f32),
            jax.ShapeDtypeStruct((8, rows), f32),
        ),
        in_specs=[pl.BlockSpec((chunk, F), lambda i: (i, 0)), whole, whole, whole, whole, whole],
        out_specs=(whole, whole),
        scratch_shapes=[
            pltpu.VMEM((option_rows, chunk), jnp.bfloat16),
            pltpu.VMEM((3 * places, chunk), jnp.bfloat16),
            pltpu.VMEM((3 * places, chunk), jnp.bfloat16),
            pltpu.VMEM((places, chunk), jnp.bfloat16),
            pltpu.VMEM((places, chunk), jnp.bfloat16),
            pltpu.VMEM((pieces, n_inst, rows, chunk), jnp.bfloat16),
            pltpu.SemaphoreType.DMA((stages, pieces)),
            pltpu.SemaphoreType.DMA((stages, pieces)),
            pltpu.VMEM((scen_stages + 1, 8, rows), f32),
            pltpu.VMEM((scen_stages, 8, rows), f32),
            pltpu.SemaphoreType.DMA((scen_stages,)),
            pltpu.SemaphoreType.DMA((scen_stages,)),
        ]
        + [pltpu.VMEM(size, jnp.bfloat16) for size in sizes]
        + [pltpu.VMEM(size, jnp.bfloat16) for size in sizes[1:]]
        + [pltpu.VMEM(size, f32) for size in sizes[1:]],
        compiler_params=pltpu.CompilerParams(
            vmem_limit_bytes=24 * 1024 * 1024, collective_id=0, has_side_effects=True
        ),
        cost_estimate=pl.CostEstimate(
            flops=60 * option_rows * scen_cols * 64, bytes_accessed=8 << 20, transcendentals=0
        ),
    )(factor_returns, loads, base, expand, params, held)
    margin = top[0]
    return (losses, margin)


def solution(mesh):
    return jax.shard_map(
        body,
        mesh=mesh,
        in_specs=(
            P("scen", None),
            P("inst", None),
            P(None, "inst"),
            P(),
            P(),
            P("inst"),
            P("inst"),
            P(None, "inst"),
        ),
        out_specs=(P("inst", "scen"), P("inst")),
        check_vma=False,
    )
```
